32 devices in a mesh: row: 8 (over y, x, core), col: 4 (over z).
Axes of the slice: x: 2, y: 2, z: 4, core: 2. Of those that a mesh axis runs over, the one named last changes fastest.
Arguments:
- amplitudes: bfloat16 [6144, 4096], P(('row', 'col')), may hold values from -4 to 4
- integrals: bfloat16 [4096, 4096], P('col', 'row'), may hold values from -0.25 to 0.25
- block_irrep: int32 [32], replicated, may hold values from 0 to 7
- occ_energy: float32 [6144], P('row'), may hold values from -6 to -2
- vir_energy: float32 [4096], P('col'), may hold values from 1 to 4
Outputs:
- new_amplitudes: float32 [6144, 4096], P('row', 'col')
The draws below stay inside these ranges and needn't reach their ends.
All inputs are finite; a program needn't handle non-finite values.
Results may differ from the reference program's by a relative error of at most 0.0003.
Values may be sent and summed in bfloat16 or wider, within the bound.
A program may use at most 128 MiB of HBM per device.

```python
import jax
import jax.numpy as jnp

VB = 128
BLOCKS = 32
CD = 4096
PAIRS = 6144


def plant(entries, rng, low, high):
    longest = entries.shape.index(max(entries.shape))
    spots = []
    for shift in (0, 1):
        where = [jax.random.randint(jax.random.fold_in(rng, axis), (), 0, length) for axis, length in enumerate(entries.shape)]
        where[longest] = (where[longest] + shift) % entries.shape[longest]
        spots.append(tuple(where))
    return entries.at[spots[0]].set(low).at[spots[1]].set(high)


def steps_of(stream_key, dims, shards, low, largest):
    factor_of, own = 1.0, jax.random.fold_in(stream_key, 6)
    for position, shards_of in shards:
        steps = jnp.exp(jax.random.uniform(jax.random.fold_in(own, position), (shards_of,), jnp.float32, low / len(shards), largest / len(shards)))
        factor_of = factor_of * jnp.repeat(steps, dims[position] // shards_of).reshape([-1 if axis == position else 1 for axis in range(len(dims))])
    return factor_of


def normal_values(stream_key, dims, deviation, bound, shards=(), held_as=jnp.bfloat16):
    drawn = jax.random.normal(stream_key, dims, jnp.float32) * deviation
    if len(shards) > 0:
        drawn = steps_of(stream_key, dims, shards, -0.22, 0.18) * drawn
    return jnp.clip(drawn, min=-bound, max=bound).astype(held_as)


def setup_inputs(seed: int = 0) -> dict:
    keys = jax.random.split(jax.random.key(seed), 6)
    return {
        "amplitudes": normal_values(keys[0], (PAIRS, CD), 0.5, 4.0, ((0, 32),)),
        "integrals": normal_values(keys[1], (CD, CD), (CD // 8) ** -0.5, 0.25, ((0, 4), (1, 8))),
        "block_irrep": plant(jax.random.randint(keys[2], (BLOCKS,), 0, 8), jax.random.fold_in(keys[2], 1), 0, 7).astype(jnp.int32),
        "occ_energy": jnp.clip(-6.0 + 4.0 * jax.random.uniform(keys[3], (PAIRS,), jnp.float32) ** steps_of(keys[3], (PAIRS,), ((0, 8),), -0.2, 0.2), -6.0, -2.0),
        "vir_energy": jnp.clip(1.0 + 3.0 * jax.random.uniform(keys[4], (CD,), jnp.float32) ** steps_of(keys[4], (CD,), ((0, 4),), -0.2, 0.2), 1.0, 4.0),
    }


def reference(amplitudes, integrals, block_irrep, occ_energy, vir_energy):
    irrep = jnp.repeat(block_irrep, VB)
    same = irrep[:, None] == irrep[None, :]
    masked = jnp.where(same, integrals, jnp.zeros_like(integrals))
    ladder = jnp.dot(amplitudes, masked.T, preferred_element_type=jnp.float32)
    denom = occ_energy[:, None] - vir_energy[None, :]
    return amplitudes.astype(jnp.float32) + ladder / denom
```

```python
import functools

import jax
import jax.numpy as jnp
from jax import lax
from jax.experimental import pallas as pl
from jax.experimental.pallas import tpu as pltpu
from jax.sharding import PartitionSpec as P

VB = 128
MESH = pl.DeviceIdType.MESH


def by_collectives(amplitudes, integrals, block_irrep, occ_energy, vir_energy):
    ab_local = integrals.shape[0]
    ab_start = lax.axis_index("col") * ab_local
    irrep = jnp.repeat(block_irrep, VB)
    row_irrep = lax.dynamic_slice_in_dim(irrep, ab_start, ab_local)
    whole_amps = lax.all_gather(amplitudes, "col", axis=0, tiled=True)
    piece = lax.all_gather(integrals, "row", axis=1, tiled=True)
    keep = row_irrep[:, None] == irrep[None, :]
    ladder = lax.dot_general(
        whole_amps,
        jnp.where(keep, piece, jnp.zeros_like(piece)),
        (((1,), (1,)), ((), ())),
        preferred_element_type=jnp.float32,
    )
    own = lax.dynamic_slice_in_dim(whole_amps, ab_start, ab_local, 1).astype(jnp.float32)
    return own + ladder / (occ_energy[:, None] - vir_energy[None, :])


def kernel(ij, ab, cd, amps_hbm, itg_hbm, keep_ref, keep_far_ref, occ_ref, vir_ref, out_hbm,
           amp, itg, far, masked, acc, res, vir_far,
           load_a, load_i, store, up_s, up_r, dn_s, dn_r,
           i_s, i_r, f_s, f_r, j_s, j_r, v_s, v_r, res_s, res_r):
    r = lax.axis_index("row")
    z = lax.axis_index("col")
    core, x, y = r % 2, (r // 2) % 2, r // 4
    half = ab // 2
    inner = jnp.logical_and(z > 0, z < 3)

    def other(k):
        return ((y + k // 4) % 2) * 4 + ((x + (k // 2) % 2) % 2) * 2 + (core + k % 2) % 2

    barrier = pltpu.get_barrier_semaphore()
    for k in (1, 2, 4):
        pl.semaphore_signal(barrier, inc=1, device_id=(other(k), z), device_id_type=MESH)

    @pl.when(z < 3)
    def _():
        pl.semaphore_signal(barrier, inc=1, device_id=(r, z + 1), device_id_type=MESH)

    @pl.when(z > 0)
    def _():
        pl.semaphore_signal(barrier, inc=1, device_id=(r, z - 1), device_id_type=MESH)

    def load_amps(c):
        return pltpu.make_async_copy(amps_hbm.at[:, pl.ds(c * cd, cd)], amp.at[z, c], load_a.at[c])

    loads = [load_amps(c) for c in range(8)]
    load_itg = pltpu.make_async_copy(itg_hbm, itg.at[0], load_i)
    load_itg.start()
    for copy in loads:
        copy.start()
    load_itg.wait()
    for copy in loads:
        copy.wait()

    @pl.when(inner)
    def _():
        pl.semaphore_wait(barrier, 5)

    @pl.when(jnp.logical_not(inner))
    def _():
        pl.semaphore_wait(barrier, 4)

    def up(s, k):
        c = other(k)
        return pltpu.make_async_remote_copy(
            amp.at[z - s, c], amp.at[z - s, c], up_s.at[s, k], up_r.at[s, k],
            device_id=(r, z + 1), device_id_type=MESH)

    def up_in(s, k):
        c = other(k)
        return pltpu.make_async_remote_copy(
            amp.at[z - 1 - s, c], amp.at[z - 1 - s, c], up_s.at[s, k], up_r.at[s, k],
            device_id=(r, z - 1), device_id_type=MESH)

    def dn(s, k):
        c = other(k)
        return pltpu.make_async_remote_copy(
            amp.at[z + s, c], amp.at[z + s, c], dn_s.at[s, k], dn_r.at[s, k],
            device_id=(r, z - 1), device_id_type=MESH)

    def dn_in(s, k):
        c = other(k)
        return pltpu.make_async_remote_copy(
            amp.at[z + 1 + s, c], amp.at[z + 1 + s, c], dn_s.at[s, k], dn_r.at[s, k],
            device_id=(r, z + 1), device_id_type=MESH)

    def sends_up(s):
        return jnp.logical_and(z >= s, z < 2) if s == 0 else jnp.logical_and(z >= s, z < 3)

    def gets_up(s):
        return jnp.logical_and(z >= 1 + s, z < 3) if s == 0 else z >= 1 + s

    def sends_dn(s):
        return z >= 2 if s == 0 else jnp.logical_and(z > 0, z <= 3 - s)

    def gets_dn(s):
        return jnp.logical_and(z > 0, z <= 2) if s == 0 else z <= 2 - s

    def pass_on(s, k):
        @pl.when(gets_up(s))
        def _():
            up_in(s, k).wait_recv()
        if s < 2:
            @pl.when(sends_up(s + 1))
            def _():
                up(s + 1, k).start()

        @pl.when(gets_dn(s))
        def _():
            dn_in(s, k).wait_recv()
        if s < 2:
            @pl.when(sends_dn(s + 1))
            def _():
                dn(s + 1, k).start()

    def exchange(buf, send, recv):
        def part(k, h):
            return buf.at[k, pl.ds(h * half, half), :]

        def copy(k, h, to):
            return pltpu.make_async_remote_copy(
                part(k, h), part(k ^ to, h), send.at[to // 2, k, h], recv.at[k ^ to, h],
                device_id=(other(to), z), device_id_type=MESH)

        def arrived(k, h):
            pltpu.make_async_remote_copy(
                part(k, h), part(k, h), send.at[0, k, h], recv.at[k, h],
                device_id=(other(1), z), device_id_type=MESH).wait_recv()

        def first():
            for h in (0, 1):
                copy(0, h, 2).start()
                copy(0, h, 4).start()
                copy(0, h, 1).start()

        def second(h):
            arrived(2, h)
            arrived(4, h)
            if h == 0:
                copy(2, 0, 4).start()
            else:
                copy(4, 1, 2).start()
            copy(2, h, 1).start()
            copy(4, h, 1).start()

        def third():
            for h in (0, 1):
                arrived(6, h)
                copy(6, h, 1).start()

        def last():
            for h in (0, 1):
                for k in (1, 3, 5, 7):
                    arrived(k, h)

        def sent():
            for h in (0, 1):
                for to in (2, 4, 1):
                    copy(0, h, to).wait_send()
                for k in (2, 4, 6):
                    copy(k, h, 1).wait_send()
            copy(2, 0, 4).wait_send()
            copy(4, 1, 2).wait_send()

        return first, second, third, last, sent

    first, second, third, last, sent = exchange(itg, i_s, i_r)
    far_first, far_second, far_third, far_last, far_sent = exchange(far, f_s, f_r)

    inward = jnp.where(z == 0, 1, 2)

    def lend(h):
        return pltpu.make_async_remote_copy(
            itg.at[0, pl.ds(h * half, half), :], far.at[0, pl.ds(h * half, half), :],
            j_s.at[h], j_r.at[h], device_id=(r, inward), device_id_type=MESH)

    lend_vir = pltpu.make_async_remote_copy(
        vir_ref, vir_far, v_s, v_r, device_id=(r, inward), device_id_type=MESH)
    outward = jnp.where(z == 1, 0, 3)

    def give(h):
        s = pl.ds(h * (ij // 2), ij // 2)
        return pltpu.make_async_remote_copy(
            res.at[s, :], acc.at[z, s, :], res_s.at[h], res_r.at[h],
            device_id=(r, outward), device_id_type=MESH)

    @pl.when(jnp.logical_not(inner))
    def _():
        lend(0).start()
        lend(1).start()
        lend_vir.start()

    first()

    def own_out(k, carry):
        @pl.when(sends_up(0))
        def _():
            up(0, k).start()

        @pl.when(sends_dn(0))
        def _():
            dn(0, k).start()
        return carry

    lax.fori_loop(0, 8, own_out, 0)

    def has(q):
        away = jnp.where(q > z, q - z, z - q)
        near = jnp.where(inner, away >= 0, away != 1)
        return jnp.logical_and(near, away <= 2)

    def mask(buf, keep, k):
        c = other(k)
        for j in range(ab // VB):
            rows = pl.ds(j * VB, VB)
            m = keep[c, pl.ds(j, 1), :].astype(jnp.bfloat16)
            masked[k, rows, :] = buf[k, rows, :] * jnp.broadcast_to(m, (VB, cd))

    def term(q, k):
        return lax.dot_general(amp[q, other(k)], masked[k], (((1,), (1,)), ((), ())),
                               preferred_element_type=jnp.float32)

    def finish(q, target, total, vir, plane):
        for h in range(ab // cd):
            cols = pl.ds(h * cd, cd)
            own = amp[q, plane * (ab // cd) + h].astype(jnp.float32)
            target[:, cols] = own + total[:, cols] / (occ_ref[q] - vir[:, cols])

    def phase(s, lo, hi):
        def step(k, carry):
            pass_on(s, k)
            return carry
        lax.fori_loop(lo, hi, step, 0)

    phase(0, 0, 3)
    second(0)
    phase(0, 3, 6)
    second(1)
    phase(0, 6, 8)

    @pl.when(inner)
    def _():
        lend(0).wait_recv()
        lend(1).wait_recv()
        pltpu.make_async_remote_copy(
            vir_ref, vir_far, v_s, v_r, device_id=(r, inward), device_id_type=MESH).wait_recv()
        far_first()

    third()
    last()

    def multiply(k, carry):
        pass_on(1, k)
        mask(itg, keep_ref, k)

        def row_block(q, carry):
            @pl.when(has(q))
            def _():
                @pl.when(k == 0)
                def _():
                    acc[q] = term(q, k)

                @pl.when(k > 0)
                def _():
                    acc[q] += term(q, k)
            return carry

        lax.fori_loop(0, 4, row_block, 0)
        return carry

    lax.fori_loop(0, 3, multiply, 0)
    pl.when(inner)(lambda: far_second(0))
    lax.fori_loop(3, 6, multiply, 0)
    pl.when(inner)(lambda: far_second(1))
    lax.fori_loop(6, 8, multiply, 0)

    def put(q):
        return pltpu.make_async_copy(acc.at[q], out_hbm.at[pl.ds(q * ij, ij), :], store.at[q])

    def close(q, carry):
        @pl.when(has(q))
        def _():
            finish(q, acc.at[q], acc.at[q], vir_ref, z)
            put(q).start()
        return carry

    lax.fori_loop(0, 4, close, 0)

    @pl.when(inner)
    def _():
        far_third()

        def far_step(k, carry):
            mask(far, keep_far_ref, k)

            @pl.when(k == 0)
            def _():
                res[...] = term(z, k)

            @pl.when(k > 0)
            def _():
                res[...] += term(z, k)
            return carry

        far_last()
        lax.fori_loop(0, 8, far_step, 0)
        finish(z, res, res, vir_far, outward)
        give(0).start()
        give(1).start()
        far_sent()
        give(0).wait_send()
        give(1).wait_send()

    @pl.when(jnp.logical_not(inner))
    def _():
        q = 3 - z

        def step(k, carry):
            pass_on(2, k)

            @pl.when(k == 0)
            def _():
                acc[q] = term(q, k)

            @pl.when(k > 0)
            def _():
                acc[q] += term(q, k)
            return carry

        lax.fori_loop(0, 8, step, 0)
        finish(q, acc.at[q], acc.at[q], vir_ref, z)
        put(q).start()
        lend(0).wait_send()
        lend(1).wait_send()
        lend_vir.wait_send()
        for h in (0, 1):
            s = pl.ds(h * (ij // 2), ij // 2)
            pltpu.make_async_remote_copy(
                res.at[s, :], acc.at[inward, s, :], res_s.at[h], res_r.at[h],
                device_id=(r, inward), device_id_type=MESH).wait_recv()
        put(inward).start()

    sent()

    def drained(k, carry):
        for s in (0, 1, 2):
            @pl.when(sends_up(s))
            def _():
                up(s, k).wait_send()

            @pl.when(sends_dn(s))
            def _():
                dn(s, k).wait_send()
        return carry

    lax.fori_loop(0, 8, drained, 0)
    for q in range(4):
        put(q).wait()


def by_kernel(amplitudes, integrals, block_irrep, occ_energy, vir_energy):
    ij, all_cd = amplitudes.shape
    ab, cd = integrals.shape
    z = lax.axis_index("col")
    blocks = ab // VB
    columns = jnp.repeat(block_irrep, VB).reshape(8, 1, cd)

    def keep_of(plane):
        rows = lax.dynamic_slice_in_dim(block_irrep, plane * blocks, blocks)
        return (rows[None, :, None] == columns).astype(jnp.float32)

    vmem = pl.BlockSpec(memory_space=pltpu.VMEM)
    hbm = pl.BlockSpec(memory_space=pl.ANY)
    bf16, f32, dma = jnp.bfloat16, jnp.float32, pltpu.SemaphoreType.DMA
    return pl.pallas_call(
        functools.partial(kernel, ij, ab, cd),
        out_shape=jax.ShapeDtypeStruct((4 * ij, ab), f32),
        in_specs=[hbm, hbm, vmem, vmem, vmem, vmem],
        out_specs=hbm,
        scratch_shapes=[
            pltpu.VMEM((4, 8, ij, cd), bf16),
            pltpu.VMEM((8, ab, cd), bf16),
            pltpu.VMEM((8, ab, cd), bf16),
            pltpu.VMEM((8, ab, cd), bf16),
            pltpu.VMEM((4, ij, ab), f32),
            pltpu.VMEM((ij, ab), f32),
            pltpu.VMEM((1, ab), f32),
            dma((8,)), dma, dma((4,)),
            dma((3, 8)), dma((3, 8)), dma((3, 8)), dma((3, 8)),
            dma((3, 8, 2)), dma((8, 2)), dma((3, 8, 2)), dma((8, 2)),
            dma((2,)), dma((2,)), dma, dma, dma((2,)), dma((2,)),
        ],
        compiler_params=pltpu.CompilerParams(
            collective_id=0, has_side_effects=True, vmem_limit_bytes=56 * 2**20),
        cost_estimate=pl.CostEstimate(
            flops=10 * ij * ab * all_cd, bytes_accessed=8 * ij * ab * 4, transcendentals=0),
    )(amplitudes, integrals, keep_of(z), keep_of(3 * lax.shift_right_logical(z, 1)),
      occ_energy.reshape(4, ij, 1), vir_energy.reshape(1, ab))


def solution(mesh):
    line = mesh.shape["row"] == 8 and mesh.shape["col"] == 4
    return jax.shard_map(
        by_kernel if line else by_collectives,
        mesh=mesh,
        in_specs=(P(("row", "col"), None), P("col", "row"), P(), P("row"), P("col")),
        out_specs=P("row", "col"),
        check_vma=False,
    )
```

```python
import functools

import jax
import jax.numpy as jnp
from jax import lax
from jax.experimental import pallas as pl
from jax.experimental.pallas import tpu as pltpu
from jax.sharding import PartitionSpec as P

VB = 128
MESH = pl.DeviceIdType.MESH


def by_collectives(amplitudes, integrals, block_irrep, occ_energy, vir_energy):
    ab_local = integrals.shape[0]
    ab_start = lax.axis_index("col") * ab_local
    irrep = jnp.repeat(block_irrep, VB)
    row_irrep = lax.dynamic_slice_in_dim(irrep, ab_start, ab_local)
    whole_amps = lax.all_gather(amplitudes, "col", axis=0, tiled=True)
    piece = lax.all_gather(integrals, "row", axis=1, tiled=True)
    keep = row_irrep[:, None] == irrep[None, :]
    ladder = lax.dot_general(
        whole_amps,
        jnp.where(keep, piece, jnp.zeros_like(piece)),
        (((1,), (1,)), ((), ())),
        preferred_element_type=jnp.float32,
    )
    own = lax.dynamic_slice_in_dim(whole_amps, ab_start, ab_local, 1).astype(jnp.float32)
    return own + ladder / (occ_energy[:, None] - vir_energy[None, :])


def kernel(ij, ab, cd, amps_hbm, itg_hbm, irrep_ref, occ_ref, vir_ref, out_hbm,
           amp, itg, far, masked, acc, res, vir_far, occ_rows,
           load_a, load_i, store, up_s, up_r,
           i_s, i_r, f_s, f_r, j_s, j_r, v_s, v_r, res_s, res_r):
    r = lax.axis_index("row")
    z = lax.axis_index("col")
    core, x, y = r % 2, (r // 2) % 2, r // 4
    half = ab // 2
    inner = jnp.logical_and(z > 0, z < 3)

    def other(k):
        return ((y + k // 4) % 2) * 4 + ((x + (k // 2) % 2) % 2) * 2 + (core + k % 2) % 2

    barrier = pltpu.get_barrier_semaphore()
    for k in (1, 2, 4):
        pl.semaphore_signal(barrier, inc=1, device_id=(other(k), z), device_id_type=MESH)

    @pl.when(z < 3)
    def _():
        pl.semaphore_signal(barrier, inc=1, device_id=(r, z + 1), device_id_type=MESH)

    @pl.when(z > 0)
    def _():
        pl.semaphore_signal(barrier, inc=1, device_id=(r, z - 1), device_id_type=MESH)

    def load_amps(c):
        return pltpu.make_async_copy(amps_hbm.at[:, pl.ds(c * cd, cd)], amp.at[z, c], load_a.at[c])

    loads = [load_amps(c) for c in range(8)]
    load_itg = pltpu.make_async_copy(itg_hbm, itg.at[0], load_i)
    load_itg.start()
    for copy in loads:
        copy.start()
    load_itg.wait()
    for copy in loads:
        copy.wait()

    @pl.when(inner)
    def _():
        pl.semaphore_wait(barrier, 5)

    @pl.when(jnp.logical_not(inner))
    def _():
        pl.semaphore_wait(barrier, 4)

    def move(q, k, to, way):
        c = other(k)
        return pltpu.make_async_remote_copy(
            amp.at[q, c], amp.at[q, c], up_s.at[way, q, k], up_r.at[q, k],
            device_id=(r, to), device_id_type=MESH)

    def exchange(buf, send, recv):
        def part(k, h):
            return buf.at[k, pl.ds(h * half, half), :]

        def copy(k, h, to):
            return pltpu.make_async_remote_copy(
                part(k, h), part(k ^ to, h), send.at[to // 2, k, h], recv.at[k ^ to, h],
                device_id=(other(to), z), device_id_type=MESH)

        def arrived(k, h):
            pltpu.make_async_remote_copy(
                part(k, h), part(k, h), send.at[0, k, h], recv.at[k, h],
                device_id=(other(1), z), device_id_type=MESH).wait_recv()

        def first():
            for h in (0, 1):
                copy(0, h, 2).start()
                copy(0, h, 4).start()
                copy(0, h, 1).start()

        def second(h):
            arrived(2, h)
            arrived(4, h)
            if h == 0:
                copy(2, 0, 4).start()
            else:
                copy(4, 1, 2).start()
            copy(2, h, 1).start()
            copy(4, h, 1).start()

        def third():
            for h in (0, 1):
                arrived(6, h)
                copy(6, h, 1).start()

        def last(*which):
            for h in (0, 1):
                for k in which:
                    arrived(k, h)

        def sent():
            for h in (0, 1):
                for to in (2, 4, 1):
                    copy(0, h, to).wait_send()
                for k in (2, 4, 6):
                    copy(k, h, 1).wait_send()
            copy(2, 0, 4).wait_send()
            copy(4, 1, 2).wait_send()

        return first, second, third, last, sent

    first, second, third, last, sent = exchange(itg, i_s, i_r)
    far_first, far_second, far_third, far_last, far_sent = exchange(far, f_s, f_r)

    inward = jnp.where(z == 0, 1, 2)
    outward = jnp.where(z == 1, 0, 3)
    peer = 3 - z

    def lend(h):
        return pltpu.make_async_remote_copy(
            itg.at[0, pl.ds(h * half, half), :], far.at[0, pl.ds(h * half, half), :],
            j_s.at[h], j_r.at[h], device_id=(r, inward), device_id_type=MESH)

    lend_vir = pltpu.make_async_remote_copy(
        vir_ref, vir_far, v_s, v_r, device_id=(r, inward), device_id_type=MESH)

    def give(h, q, to):
        s = pl.ds(h * (ij // 2), ij // 2)
        return pltpu.make_async_remote_copy(
            res.at[s, :], acc.at[q, s, :], res_s.at[h], res_r.at[h],
            device_id=(r, to), device_id_type=MESH)

    def loop(lo, hi, body):
        def step(k, carry):
            body(k)
            return carry
        lax.fori_loop(lo, hi, step, 0)

    lane_block = lax.broadcasted_iota(jnp.int32, (1, cd), 1) // VB
    per = cd // VB

    def mask(buf, plane, k):
        c = other(k)
        columns = [irrep_ref[c * per + i] for i in range(per)]
        for j in range(ab // VB):
            line = irrep_ref[plane * (ab // VB) + j]
            m = jnp.zeros((1, cd), jnp.float32)
            for i in range(per):
                same = jnp.where(columns[i] == line, 1.0, 0.0).astype(jnp.float32)
                m = jnp.where(lane_block == i, same, m)
            rows = pl.ds(j * VB, VB)
            masked[k, rows, :] = buf[k, rows, :] * jnp.broadcast_to(m.astype(jnp.bfloat16), (VB, cd))

    def term(q, k):
        return lax.dot_general(amp[q, other(k)], masked[k], (((1,), (1,)), ((), ())),
                               preferred_element_type=jnp.float32)

    def add(q, k):
        @pl.when(k == 0)
        def _():
            acc[q] = term(q, k)

        @pl.when(k > 0)
        def _():
            acc[q] += term(q, k)

    def far_add(*which):
        for k in which:
            mask(far, outward, k)
            if k == 0:
                res[...] = term(z, k)
            else:
                res[...] += term(z, k)

    def finish(q, target, vir, plane):
        rows = pl.ds(pl.multiple_of(q * ij, 8), ij)
        for h in range(ab // cd):
            cols = pl.ds(h * cd, cd)
            own = amp[q, plane * (ab // cd) + h].astype(jnp.float32)
            target[:, cols] = own + target[:, cols] / (occ_rows[rows, :1] - vir[:, cols])

    def put(q):
        return pltpu.make_async_copy(acc.at[q], out_hbm.at[pl.ds(q * ij, ij), :], store.at[q])

    def close(q):
        finish(q, acc.at[q], vir_ref, z)
        put(q).start()

    def flip():
        occ_rows[...] = jnp.transpose(jnp.broadcast_to(occ_ref[...], (VB, 4 * ij)))

    @pl.when(inner)
    def _():
        first()
        loop(0, 8, lambda k: move(z, k, peer, 1).start())
        flip()

        def from_peer(k):
            move(peer, k, peer, 0).wait_recv()
            move(peer, k, outward, 0).start()

        def from_end(k):
            move(outward, k, outward, 1).wait_recv()
            move(outward, k, peer, 1).start()

        def from_far(k):
            move(3 - outward, k, peer, 0).wait_recv()
            move(3 - outward, k, outward, 0).start()

        def both(k):
            mask(itg, z, k)
            add(z, k)
            add(peer, k)

        loop(0, 2, from_peer)
        second(0)
        loop(2, 5, from_peer)
        second(1)
        for h in (0, 1):
            pltpu.make_async_remote_copy(
                far.at[0, pl.ds(h * half, half), :], far.at[0, pl.ds(h * half, half), :],
                j_s.at[h], j_r.at[h], device_id=(r, outward), device_id_type=MESH).wait_recv()
        pltpu.make_async_remote_copy(
            vir_ref, vir_far, v_s, v_r, device_id=(r, outward), device_id_type=MESH).wait_recv()
        far_first()
        loop(5, 8, lambda k: (from_peer(k), from_end(k - 5)))
        third()
        from_end(3)
        from_far(0)
        last(1, 3, 5, 7)
        loop(0, 3, lambda k: (from_end(k + 4), from_far(k + 1), both(2 * k), both(2 * k + 1)))
        far_second(0)
        from_end(7)
        from_far(4)
        loop(6, 8, both)
        far_second(1)
        loop(0, 4, lambda k: add(outward, k))
        from_far(5)
        sent()
        loop(4, 8, lambda k: add(outward, k))
        close(z)
        close(peer)
        close(outward)
        from_far(6)
        far_add(0, 2, 4)
        far_last(1, 3, 5)
        far_add(1, 3, 5)
        from_far(7)
        far_third()
        far_add(6)
        far_last(7)
        far_add(7)
        finish(z, res, vir_far, outward)
        give(0, z, outward).start()
        give(1, z, outward).start()
        loop(0, 8, lambda k: mask(itg, z, k))
        loop(0, 8, lambda k: add(3 - outward, k))
        close(3 - outward)
        far_sent()

        def drain(k):
            move(z, k, peer, 1).wait_send()
            move(peer, k, outward, 0).wait_send()
            move(outward, k, peer, 1).wait_send()
            move(3 - outward, k, outward, 0).wait_send()

        loop(0, 8, drain)
        give(0, z, outward).wait_send()
        give(1, z, outward).wait_send()
        for q in range(4):
            put(q).wait()

    @pl.when(jnp.logical_not(inner))
    def _():
        next_one = 3 - inward
        lend(0).start()
        lend(1).start()
        lend_vir.start()
        first()
        flip()
        second(0)
        lend(0).wait_send()
        loop(0, 2, lambda k: move(z, k, inward, 1).start())
        lend(1).wait_send()
        loop(2, 8, lambda k: move(z, k, inward, 1).start())
        second(1)
        third()
        last(1, 3, 5, 7)

        def near(k):
            mask(itg, z, k)
            add(z, k)
            move(next_one, k, inward, 0).wait_recv()
            add(next_one, k)

        loop(0, 8, near)
        close(z)
        close(next_one)
        sent()
        lend_vir.wait_send()

        def end(k):
            move(peer, k, inward, 0).wait_recv()
            add(peer, k)

        loop(0, 8, end)
        close(peer)
        loop(0, 8, lambda k: move(z, k, inward, 1).wait_send())
        give(0, inward, inward).wait_recv()
        give(1, inward, inward).wait_recv()
        put(inward).start()
        for q in range(4):
            put(q).wait()


def by_kernel(amplitudes, integrals, block_irrep, occ_energy, vir_energy):
    ij, all_cd = amplitudes.shape
    ab, cd = integrals.shape
    vmem = pl.BlockSpec(memory_space=pltpu.VMEM)
    hbm = pl.BlockSpec(memory_space=pl.ANY)
    bf16, f32, dma = jnp.bfloat16, jnp.float32, pltpu.SemaphoreType.DMA
    return pl.pallas_call(
        functools.partial(kernel, ij, ab, cd),
        out_shape=jax.ShapeDtypeStruct((4 * ij, ab), f32),
        in_specs=[hbm, hbm, pl.BlockSpec(memory_space=pltpu.SMEM), vmem, vmem],
        out_specs=hbm,
        scratch_shapes=[
            pltpu.VMEM((4, 8, ij, cd), bf16),
            pltpu.VMEM((8, ab, cd), bf16),
            pltpu.VMEM((8, ab, cd), bf16),
            pltpu.VMEM((8, ab, cd), bf16),
            pltpu.VMEM((4, ij, ab), f32),
            pltpu.VMEM((ij, ab), f32),
            pltpu.VMEM((1, ab), f32),
            pltpu.VMEM((4 * ij, VB), f32),
            dma((8,)), dma, dma((4,)),
            dma((2, 4, 8)), dma((4, 8)),
            dma((3, 8, 2)), dma((8, 2)), dma((3, 8, 2)), dma((8, 2)),
            dma((2,)), dma((2,)), dma, dma, dma((2,)), dma((2,)),
        ],
        compiler_params=pltpu.CompilerParams(
            collective_id=0, has_side_effects=True, vmem_limit_bytes=40 * 2**20),
        cost_estimate=pl.CostEstimate(
            flops=10 * ij * ab * all_cd, bytes_accessed=8 * ij * ab * 4, transcendentals=0),
    )(amplitudes, integrals, block_irrep, occ_energy.reshape(1, 4 * ij), vir_energy.reshape(1, ab))


def solution(mesh):
    line = mesh.shape["row"] == 8 and mesh.shape["col"] == 4
    return jax.shard_map(
        by_kernel if line else by_collectives,
        mesh=mesh,
        in_specs=(P(("row", "col"), None), P("col", "row"), P(), P("row"), P("col")),
        out_specs=P("row", "col"),
        check_vma=False,
    )
```

```python
import functools

import jax
import jax.numpy as jnp
from jax import lax
from jax.experimental import pallas as pl
from jax.experimental.pallas import tpu as pltpu
from jax.sharding import PartitionSpec as P

VB = 128
MESH = pl.DeviceIdType.MESH


def by_collectives(amplitudes, integrals, block_irrep, occ_energy, vir_energy):
    ab_local = integrals.shape[0]
    ab_start = lax.axis_index("col") * ab_local
    irrep = jnp.repeat(block_irrep, VB)
    row_irrep = lax.dynamic_slice_in_dim(irrep, ab_start, ab_local)
    whole_amps = lax.all_gather(amplitudes, "col", axis=0, tiled=True)
    piece = lax.all_gather(integrals, "row", axis=1, tiled=True)
    keep = row_irrep[:, None] == irrep[None, :]
    ladder = lax.dot_general(
        whole_amps,
        jnp.where(keep, piece, jnp.zeros_like(piece)),
        (((1,), (1,)), ((), ())),
        preferred_element_type=jnp.float32,
    )
    own = lax.dynamic_slice_in_dim(whole_amps, ab_start, ab_local, 1).astype(jnp.float32)
    return own + ladder / (occ_energy[:, None] - vir_energy[None, :])


def kernel(ij, ab, cd, amps_hbm, itg_hbm, irrep_hbm, occ_ref, vir_ref, out_hbm,
           irrep_ref, amp, itg, far, masked, masked_far, acc, res, vir_far, occ_rows,
           load_a, load_i, load_b, store, up_s, up_r, e_s, e_r,
           i_s, i_r, f_s, f_r, j_s, j_r, v_s, v_r, res_s, res_r):
    r = lax.axis_index("row")
    z = lax.axis_index("col")
    core, x, y = r % 2, (r // 2) % 2, r // 4
    half = ab // 2
    inner = jnp.logical_and(z > 0, z < 3)

    def other(k):
        return ((y + k // 4) % 2) * 4 + ((x + (k // 2) % 2) % 2) * 2 + (core + k % 2) % 2

    barrier = pltpu.get_barrier_semaphore()
    for k in (1, 2, 4):
        pl.semaphore_signal(barrier, inc=1, device_id=(other(k), z), device_id_type=MESH)

    @pl.when(z < 3)
    def _():
        pl.semaphore_signal(barrier, inc=1, device_id=(r, z + 1), device_id_type=MESH)

    @pl.when(z > 0)
    def _():
        pl.semaphore_signal(barrier, inc=1, device_id=(r, z - 1), device_id_type=MESH)

    def load_amps(c):
        return pltpu.make_async_copy(amps_hbm.at[:, pl.ds(c * cd, cd)], amp.at[z, c], load_a.at[c])

    loads = [load_amps(c) for c in range(8)]
    load_itg = pltpu.make_async_copy(itg_hbm, itg.at[0], load_i)
    load_itg.start()
    load_irrep = pltpu.make_async_copy(irrep_hbm, irrep_ref, load_b)
    load_irrep.start()
    for copy in loads:
        copy.start()
    load_itg.wait()
    load_irrep.wait()
    for copy in loads:
        copy.wait()

    @pl.when(inner)
    def _():
        pl.semaphore_wait(barrier, 5)

    @pl.when(jnp.logical_not(inner))
    def _():
        pl.semaphore_wait(barrier, 4)

    def move(q, k, to, way):
        c = other(k)
        return pltpu.make_async_remote_copy(
            amp.at[q, c], amp.at[q, c], up_s.at[way, q, k], up_r.at[q, k],
            device_id=(r, to), device_id_type=MESH)

    def carry_half(q, k, to, way):
        part = amp.at[q, other(k % 8), pl.ds(pl.multiple_of((k // 8) * (ij // 2), 16), ij // 2), :]
        return pltpu.make_async_remote_copy(
            part, part, e_s.at[way, k], e_r.at[way, k],
            device_id=(r, to), device_id_type=MESH)

    def exchange(buf, send, recv):
        def part(k, h):
            return buf.at[k, pl.ds(h * half, half), :]

        def copy(k, h, to):
            return pltpu.make_async_remote_copy(
                part(k, h), part(k ^ to, h), send.at[to // 2, k, h], recv.at[k ^ to, h],
                device_id=(other(to), z), device_id_type=MESH)

        def arrived(k, h):
            pltpu.make_async_remote_copy(
                part(k, h), part(k, h), send.at[0, k, h], recv.at[k, h],
                device_id=(other(1), z), device_id_type=MESH).wait_recv()

        def first(h):
            copy(0, h, 2).start()
            copy(0, h, 4).start()
            copy(0, h, 1).start()

        def second(h):
            arrived(2, h)
            arrived(4, h)
            if h == 0:
                copy(2, 0, 4).start()
            else:
                copy(4, 1, 2).start()
            copy(2, h, 1).start()
            copy(4, h, 1).start()

        def third():
            for h in (0, 1):
                arrived(6, h)
                copy(6, h, 1).start()

        def last(*which):
            for h in (0, 1):
                for k in which:
                    arrived(k, h)

        def sent():
            for h in (0, 1):
                for to in (2, 4, 1):
                    copy(0, h, to).wait_send()
                for k in (2, 4, 6):
                    copy(k, h, 1).wait_send()
            copy(2, 0, 4).wait_send()
            copy(4, 1, 2).wait_send()

        return first, second, third, last, sent

    first, second, third, last, sent = exchange(itg, i_s, i_r)
    far_first, far_second, far_third, far_last, far_sent = exchange(far, f_s, f_r)

    inward = jnp.where(z == 0, 1, 2)
    outward = jnp.where(z == 1, 0, 3)
    peer = 3 - z

    def lend(h):
        return pltpu.make_async_remote_copy(
            itg.at[0, pl.ds(h * half, half), :], far.at[0, pl.ds(h * half, half), :],
            j_s.at[h], j_r.at[h], device_id=(r, inward), device_id_type=MESH)

    lend_vir = pltpu.make_async_remote_copy(
        vir_ref, vir_far, v_s, v_r, device_id=(r, inward), device_id_type=MESH)

    def give(n, q, to):
        s = pl.ds((n % 2) * (ij // 2), ij // 2)
        return pltpu.make_async_remote_copy(
            res.at[n // 2, s, :], acc.at[q, s, :], res_s.at[n], res_r.at[n],
            device_id=(r, to), device_id_type=MESH)

    def loop(lo, hi, body):
        def step(k, carry):
            body(k)
            return carry
        lax.fori_loop(lo, hi, step, 0)

    lane_block = lax.broadcasted_iota(jnp.int32, (1, cd), 1) // VB
    per = cd // VB

    def mask(buf, out, plane, k):
        c = other(k)
        columns = [irrep_ref[c * per + i] for i in range(per)]
        for j in range(ab // VB):
            line = irrep_ref[plane * (ab // VB) + j]
            m = jnp.zeros((1, cd), jnp.float32)
            for i in range(per):
                same = jnp.where(columns[i] == line, 1.0, 0.0).astype(jnp.float32)
                m = jnp.where(lane_block == i, same, m)
            rows = pl.ds(j * VB, VB)
            out[k, rows, :] = buf[k, rows, :] * jnp.broadcast_to(m.astype(jnp.bfloat16), (VB, cd))

    def term(q, k):
        return lax.dot_general(amp[q, other(k)], masked[k], (((1,), (1,)), ((), ())),
                               preferred_element_type=jnp.float32)

    def add(q, k):
        @pl.when(k == 0)
        def _():
            acc[q] = term(q, k)

        @pl.when(k > 0)
        def _():
            acc[q] += term(q, k)

    def far_add(*which):
        for k in which:
            mask(far, masked_far, outward, k)
            t = lax.dot_general(amp[z, other(k)], masked_far[k], (((1,), (1,)), ((), ())),
                                preferred_element_type=jnp.float32)
            if k == 0:
                res[0] = t
            else:
                res[0] += t

    def far_half(h, k):
        rows = pl.ds(h * (ij // 2), ij // 2)
        t = lax.dot_general(amp[3 - outward, other(k), rows, :], masked_far[k],
                            (((1,), (1,)), ((), ())), preferred_element_type=jnp.float32)

        @pl.when(k == 0)
        def _():
            res[1, rows, :] = t

        @pl.when(k > 0)
        def _():
            res[1, rows, :] += t

    def finish(q, target, vir, plane, first_row=0, n_rows=ij):
        rows = pl.ds(pl.multiple_of(q * ij + first_row, 8), n_rows)
        here = pl.ds(first_row, n_rows)
        for h in range(ab // cd):
            cols = pl.ds(h * cd, cd)
            own = amp[q, plane * (ab // cd) + h, here, :].astype(jnp.float32)
            target[here, cols] = own + target[here, cols] / (occ_rows[rows, :1] - vir[:, cols])

    def put(q):
        return pltpu.make_async_copy(acc.at[q], out_hbm.at[pl.ds(q * ij, ij), :], store.at[q])

    def close(q):
        finish(q, acc.at[q], vir_ref, z)
        put(q).start()

    def flip():
        occ_rows[...] = jnp.transpose(jnp.broadcast_to(occ_ref[...], (VB, 4 * ij)))

    @pl.when(inner)
    def _():
        loop(0, 8, lambda k: move(z, k, peer, 1).start())
        flip()

        def from_peer(k):
            move(peer, k, peer, 0).wait_recv()
            move(peer, k, outward, 0).start()

        def from_end(k):
            carry_half(outward, k, outward, 0).wait_recv()
            carry_half(outward, k, peer, 1).start()

        def from_far(k):
            carry_half(3 - outward, k, peer, 1).wait_recv()

        def half_of_far(h):
            loop(0, 8, lambda k: (from_far(h * 8 + k), far_half(h, k)))
            finish(3 - outward, res.at[1], vir_far, outward, h * (ij // 2), ij // 2)
            give(2 + h, 3 - outward, outward).start()

        def near(k):
            mask(itg, masked, z, k)
            add(z, k)
            add(peer, k)

        loop(0, 3, from_peer)
        for h in (0, 1):
            pltpu.make_async_remote_copy(
                far.at[0, pl.ds(h * half, half), :], far.at[0, pl.ds(h * half, half), :],
                j_s.at[h], j_r.at[h], device_id=(r, outward), device_id_type=MESH).wait_recv()
            far_first(h)
            loop(3 + 2 * h, 5 + 2 * h, from_peer)
        pltpu.make_async_remote_copy(
            vir_ref, vir_far, v_s, v_r, device_id=(r, outward), device_id_type=MESH).wait_recv()
        far_second(0)
        loop(0, 3, from_end)
        from_peer(7)
        far_second(1)
        first(0)
        first(1)
        loop(3, 6, from_end)
        far_add(0, 2, 4)
        far_last(1, 3, 5)
        far_add(1, 3, 5)
        far_third()
        far_add(6)
        far_last(7)
        far_add(7)
        finish(z, res.at[0], vir_far, outward)
        give(0, z, outward).start()
        give(1, z, outward).start()
        loop(6, 9, from_end)
        second(0)
        loop(9, 12, from_end)
        half_of_far(0)
        second(1)
        loop(12, 16, from_end)
        third()
        half_of_far(1)
        last(1, 3, 5, 7)
        loop(0, 8, near)
        close(z)
        close(peer)
        loop(0, 8, lambda k: (add(outward, k), add(3 - outward, k)))
        close(outward)
        close(3 - outward)
        sent()
        far_sent()

        def drain(k):
            move(z, k, peer, 1).wait_send()
            move(peer, k, outward, 0).wait_send()
            carry_half(outward, k, peer, 1).wait_send()
            carry_half(outward, k + 8, peer, 1).wait_send()

        loop(0, 8, drain)
        for n in range(4):
            give(n, z, outward).wait_send()
        for q in range(4):
            put(q).wait()

    @pl.when(jnp.logical_not(inner))
    def _():
        next_one = 3 - inward
        lend(0).start()
        lend(1).start()
        lend_vir.start()
        first(0)
        first(1)
        flip()
        second(0)
        lend(0).wait_send()
        loop(0, 3, lambda k: carry_half(z, k, inward, 0).start())
        lend(1).wait_send()
        loop(3, 16, lambda k: carry_half(z, k, inward, 0).start())
        second(1)
        third()
        last(1, 3, 5, 7)

        def near(k):
            mask(itg, masked, z, k)
            add(z, k)
            move(next_one, k, inward, 0).wait_recv()
            add(next_one, k)

        loop(0, 8, near)
        close(z)
        close(next_one)
        sent()
        lend_vir.wait_send()

        loop(0, 16, lambda k: carry_half(z, k, inward, 0).wait_send())
        give(0, inward, inward).wait_recv()
        give(1, inward, inward).wait_recv()
        put(inward).start()
        give(2, peer, inward).wait_recv()
        give(3, peer, inward).wait_recv()
        put(peer).start()
        for q in range(4):
            put(q).wait()


def by_kernel(amplitudes, integrals, block_irrep, occ_energy, vir_energy):
    ij, all_cd = amplitudes.shape
    ab, cd = integrals.shape
    vmem = pl.BlockSpec(memory_space=pltpu.VMEM)
    hbm = pl.BlockSpec(memory_space=pltpu.HBM)
    bf16, f32, dma = jnp.bfloat16, jnp.float32, pltpu.SemaphoreType.DMA
    return pl.pallas_call(
        functools.partial(kernel, ij, ab, cd),
        out_shape=jax.ShapeDtypeStruct((4 * ij, ab), f32),
        in_specs=[hbm, hbm, hbm, vmem, vmem],
        out_specs=pl.BlockSpec(memory_space=pl.ANY),
        scratch_shapes=[
            pltpu.SMEM((all_cd // VB,), jnp.int32),
            pltpu.VMEM((4, 8, ij, cd), bf16),
            pltpu.VMEM((8, ab, cd), bf16),
            pltpu.VMEM((8, ab, cd), bf16),
            pltpu.VMEM((8, ab, cd), bf16),
            pltpu.VMEM((8, ab, cd), bf16),
            pltpu.VMEM((4, ij, ab), f32),
            pltpu.VMEM((2, ij, ab), f32),
            pltpu.VMEM((1, ab), f32),
            pltpu.VMEM((4 * ij, VB), f32),
            dma((8,)), dma, dma, dma((4,)),
            dma((2, 4, 8)), dma((4, 8)), dma((2, 16)), dma((2, 16)),
            dma((3, 8, 2)), dma((8, 2)), dma((3, 8, 2)), dma((8, 2)),
            dma((2,)), dma((2,)), dma, dma, dma((4,)), dma((4,)),
        ],
        compiler_params=pltpu.CompilerParams(
            collective_id=0, has_side_effects=True, vmem_limit_bytes=48 * 2**20),
        cost_estimate=pl.CostEstimate(
            flops=10 * ij * ab * all_cd, bytes_accessed=8 * ij * ab * 4, transcendentals=0),
    )(amplitudes, integrals, block_irrep, occ_energy.reshape(1, 4 * ij), vir_energy.reshape(1, ab))


def solution(mesh):
    line = mesh.shape["row"] == 8 and mesh.shape["col"] == 4
    return jax.shard_map(
        by_kernel if line else by_collectives,
        mesh=mesh,
        in_specs=(P(("row", "col"), None), P("col", "row"), P(), P("row"), P("col")),
        out_specs=P("row", "col"),
        check_vma=False,
    )
```
